1024 devices in a mesh: row: 16 (over z_hi, y, core), col: 64 (over z_lo, x).
Axes of the slice: x: 4, y: 4, z: 32 (z_hi: 2, z_lo: 16; z = z_hi * 16 + z_lo), core: 2. Of those that a mesh axis runs over, the one named last changes fastest.
Arguments:
- amplitudes: float32 [320, 45056], P('col', 'row'), may hold values from -6 to 6
- integrals: float32 [45056, 16384], P('row', 'col'), may hold values from -0.02734375 to 0.02734375
- direct_terms: float32 [320, 16384], P('row', 'col'), may hold values from -4 to 4
- occ_energy: float32 [320], P('row'), may hold values from -4 to -1
- virt_energy: float32 [16384], P('col'), may hold values from 0.5 to 4
Outputs:
- updated: float32 [320, 16384], P('row', 'col')
The draws below stay inside these ranges and needn't reach their ends.
All inputs are finite; a program needn't handle non-finite values.
Results may differ from the reference program's by a relative error of at most 0.000056.
Values sent between devices are 32-bit elements; how exact they have to be, the bound alone decides.
A program may use at most 32 MiB of HBM per device.

```python
import jax
import jax.numpy as jnp
from jax import lax

P_SIZE = 320
Q = 45056
R = 16384


def level_of(rng, shape, pieces, least, top_value):
    def one(axis_at, shards_of):
        steps = jax.random.uniform(jax.random.fold_in(jax.random.fold_in(rng, 6), axis_at), (shards_of,), jnp.float32, least / len(pieces), top_value / len(pieces))
        return jnp.repeat(jnp.exp(steps), shape[axis_at] // shards_of).reshape((-1,) + (1,) * (len(shape) - axis_at - 1))

    factor_of = one(*pieces[0])
    for cut in pieces[1:]:
        factor_of = factor_of * one(*cut)
    return factor_of


def noise(own_key, dims, scale, reach, split=(), held_as=jnp.bfloat16):
    factor_of = level_of(own_key, dims, split, -0.22, 0.18) if split else 1.0
    drawn = jax.random.normal(own_key, dims, jnp.float32) * scale * factor_of
    return jnp.minimum(jnp.maximum(drawn, -reach), reach).astype(held_as)


def setup_inputs(seed: int = 0) -> dict:
    seeds = jax.random.split(jax.random.key(seed), 6)
    return {
        "amplitudes": noise(seeds[0], (P_SIZE, Q), 1.0, 6.0, ((0, 64), (1, 16)), jnp.float32),
        "integrals": noise(seeds[1], (Q, R), Q ** -0.5, 0.02734375, ((0, 16), (1, 64)), jnp.float32),
        "direct_terms": noise(seeds[2], (P_SIZE, R), 0.5, 4.0, ((0, 16), (1, 64)), jnp.float32),
        "occ_energy": jnp.clip(-4.0 + 3.0 * jax.random.uniform(seeds[3], (P_SIZE,), jnp.float32) ** level_of(seeds[3], (P_SIZE,), ((0, 16),), -0.2, 0.2), -4.0, -1.0),
        "virt_energy": jnp.clip(0.5 + 3.5 * jax.random.uniform(seeds[4], (R,), jnp.float32) ** level_of(seeds[4], (R,), ((0, 64),), -0.2, 0.2), 0.5, 4.0),
    }


def reference(amplitudes, integrals, direct_terms, occ_energy, virt_energy):
    ladder = jnp.dot(amplitudes, integrals, precision=lax.Precision.HIGHEST, preferred_element_type=jnp.float32)
    denominator = occ_energy[:, None] - virt_energy[None, :]
    return (0.5 * ladder + direct_terms) / denominator
```

```python
import functools

import jax
import jax.numpy as jnp
from jax import lax
from jax.experimental import pallas as pl
from jax.experimental.pallas import tpu as pltpu
from jax.sharding import PartitionSpec as P

MESH = pl.DeviceIdType.MESH
NX = 4
NZ = 16
NR = 5
LANES = 128
PEERS = 8


def kernel(n_chunks, amp_ref, b_hbm, out_ref, own, slabs, b_raw, b_hi, b_lo, lhs, part, part_in, cross, cross_in,
           b_sem, z_send, z_recv, x_send, x_recv, f_send, f_recv, p_send, p_recv, c_send, c_recv):
    rows = own.shape[0]
    half = rows // 2
    row = lax.axis_index("row")
    col = lax.axis_index("col")
    x, z = lax.rem(col, NX), col // NX
    zh, me8 = row // PEERS, lax.rem(row, PEERS)
    right = z * NX + lax.rem(x + 1, NX)
    left = z * NX + lax.rem(x + NX - 1, NX)
    x_left, x_right, x_far = lax.rem(x + 3, NX), lax.rem(x + 1, NX), lax.rem(x + 2, NX)
    partner = (1 - zh) * PEERS + me8

    b_copy = pltpu.make_async_copy(b_hbm, b_raw, b_sem)
    b_copy.start()

    barrier = pltpu.get_barrier_semaphore()

    def greet(r, c):
        pl.semaphore_signal(barrier, inc=1, device_id={"row": r, "col": c}, device_id_type=MESH)

    greet(row, left)
    greet(row, right)
    for d in range(1, PEERS):
        greet(zh * PEERS + lax.rem(me8 + d, PEERS), col)
    greet(partner, col)

    @pl.when(z > 0)
    def _():
        greet(row, col - NX)

    @pl.when(z < NZ - 1)
    def _():
        greet(row, col + NX)

    for k in range(n_chunks):
        own[k * NR : (k + 1) * NR, :] = amp_ref[:, k * LANES : (k + 1) * LANES]
    if n_chunks * NR < rows:
        own[n_chunks * NR :, :] = jnp.zeros((rows - n_chunks * NR, LANES), jnp.float32)
    slabs[z, pl.ds(pl.multiple_of(x * rows, 8), rows), :] = own[...]

    ends = jnp.where(z > 0, 1, 0) + jnp.where(z < NZ - 1, 1, 0)
    pl.semaphore_wait(barrier, 2 + PEERS + ends)

    def piece(zs, xs, p):
        return slabs.at[zs, pl.ds(pl.multiple_of(xs * rows + p * half, 8), half), :]

    def z_copy(zs, p, up):
        to = jnp.minimum(col + NX, NZ * NX - 1) if up else jnp.maximum(col - NX, 0)
        ref = piece(zs, x, p)
        return pltpu.make_async_remote_copy(ref, ref, z_send.at[up, zs, p], z_recv.at[zs, p],
                                            device_id={"row": row, "col": to}, device_id_type=MESH)

    def x_copy(zs, p, to_right):
        ref = piece(zs, x, p)
        return pltpu.make_async_remote_copy(ref, ref, x_send.at[to_right, zs, p], x_recv.at[to_right, zs, p],
                                            device_id={"row": row, "col": right if to_right else left},
                                            device_id_type=MESH)

    def x_arrival(zs, p, to_right):
        ref = piece(zs, x_left if to_right else x_right, p)
        return pltpu.make_async_copy(ref, ref, x_recv.at[to_right, zs, p])

    def f_copy(zs, to_right):
        ref = piece(zs, x_left if to_right else x_right, 1 - to_right)
        return pltpu.make_async_remote_copy(ref, ref, f_send.at[to_right, zs], f_recv.at[to_right, zs],
                                            device_id={"row": row, "col": right if to_right else left},
                                            device_id_type=MESH)

    def f_arrival(zs, to_right):
        ref = piece(zs, x_far, 1 - to_right)
        return pltpu.make_async_copy(ref, ref, f_recv.at[to_right, zs])

    def p_copy(zs):
        to = zh * PEERS + lax.rem(zs, PEERS)
        return pltpu.make_async_remote_copy(part.at[zs], part_in.at[zs // PEERS, me8], p_send.at[zs],
                                            p_recv.at[zs // PEERS, me8],
                                            device_id={"row": to, "col": col}, device_id_type=MESH)

    pairs = jnp.minimum(z, NZ - 1 - z)

    def order(n):
        near = (n + 1) // 2
        near = jnp.where(lax.rem(n, 2) == 1, z - near, z + near)
        far = jnp.where(z < NZ // 2, z + n - pairs, z - n + pairs)
        return jnp.where(n <= 2 * pairs, near, far)

    def z_start(zs, p, up):
        @pl.when((z < NZ - 1) if up else (z > 0))
        def _():
            z_copy(zs, p, up).start()

    def z_step(t):
        for p in range(2):
            @pl.when(z - t >= 0)
            def _():
                z_copy(z - t, p, 1).wait_recv()
                z_start(z - t, p, 1)

            @pl.when(z + t < NZ)
            def _():
                z_copy(z + t, p, 0).wait_recv()
                z_start(z + t, p, 0)

    def x_start(zs):
        x_copy(zs, 0, 1).start()
        x_copy(zs, 1, 0).start()
        x_copy(zs, 1, 1).start()
        x_copy(zs, 0, 0).start()

    def x_forward(zs):
        x_arrival(zs, 0, 1).wait()
        f_copy(zs, 1).start()
        x_arrival(zs, 1, 0).wait()
        f_copy(zs, 0).start()

    def finish(zs):
        x_arrival(zs, 1, 1).wait()
        x_arrival(zs, 0, 0).wait()
        f_arrival(zs, 1).wait()
        f_arrival(zs, 0).wait()
        for q in range(NX // 2):
            for k in range(n_chunks):
                v = jnp.concatenate(
                    [slabs[zs, (2 * q + i) * rows + k * NR : (2 * q + i) * rows + k * NR + 8, :] for i in range(2)],
                    axis=0)
                hi = v.astype(jnp.bfloat16)
                lo = (v - hi.astype(jnp.float32)).astype(jnp.bfloat16)
                lhs[16 * q : 16 * q + 16, k * LANES : (k + 1) * LANES] = hi
                lhs[32 + 16 * q : 48 + 16 * q, k * LANES : (k + 1) * LANES] = lo
        both = jnp.dot(lhs[...], b_hi[...], preferred_element_type=jnp.float32)
        cross_term = jnp.dot(lhs[:32, :], b_lo[...], preferred_element_type=jnp.float32)
        part[zs] = both[:32] + (both[32:] + cross_term)

        @pl.when(lax.rem(zs, PEERS) != me8)
        def _():
            p_copy(zs).start()

    for p in range(2):
        z_start(z, p, 1)
        z_start(z, p, 0)
    x_start(z)

    b_copy.wait()
    depth = b_raw.shape[0]

    @pl.loop(0, depth // 256)
    def _(i):
        at = pl.ds(pl.multiple_of(i * 256, 256), 256)
        v = b_raw[at, :]
        hi = v.astype(jnp.bfloat16)
        b_hi[at, :] = hi
        b_lo[at, :] = (v - hi.astype(jnp.float32)).astype(jnp.bfloat16)

    @pl.loop(1, NZ + 2)
    def _(t):
        z_step(t)

        @pl.when(t < NZ)
        def _():
            x_start(order(t))

        @pl.when(t < NZ + 1)
        def _():
            x_forward(order(t - 1))

        @pl.when(t >= 2)
        def _():
            finish(order(t - 2))

    def total(h):
        s = part[h * PEERS + me8]
        for d in range(1, PEERS):
            q = lax.rem(me8 + d, PEERS)
            ref = part_in.at[h, q]
            pltpu.make_async_copy(ref, ref, p_recv.at[h, q]).wait()
            s = s + part_in[h, q]
        return jnp.concatenate([s[8 * i : 8 * i + NR, :] for i in range(NX)], axis=0)

    cross[...] = total(1 - zh)
    c_copy = pltpu.make_async_remote_copy(cross, cross_in, c_send, c_recv,
                                          device_id={"row": partner, "col": col}, device_id_type=MESH)
    c_copy.start()
    mine = total(zh)
    c_copy.wait_recv()
    out_ref[...] = mine + cross_in[...]
    c_copy.wait_send()

    @pl.loop(0, NZ)
    def _(zs):
        for p in range(2):
            @pl.when((z < NZ - 1) & (zs <= z))
            def _():
                z_copy(zs, p, 1).wait_send()

            @pl.when((z > 0) & (zs >= z))
            def _():
                z_copy(zs, p, 0).wait_send()

            for to_right in range(2):
                x_copy(zs, p, to_right).wait_send()
        for to_right in range(2):
            f_copy(zs, to_right).wait_send()

        @pl.when(lax.rem(zs, PEERS) != me8)
        def _():
            p_copy(zs).wait_send()


def ladder_rows(amplitudes, integrals):
    depth, width = integrals.shape
    n_chunks = depth // LANES
    rows = -(-n_chunks * NR // 16) * 16
    f32, bf16 = jnp.float32, jnp.bfloat16
    dma = pltpu.SemaphoreType.DMA
    return pl.pallas_call(
        functools.partial(kernel, n_chunks),
        out_shape=jax.ShapeDtypeStruct((NX * NR, width), f32),
        in_specs=[pl.BlockSpec(memory_space=pltpu.VMEM), pl.BlockSpec(memory_space=pl.ANY)],
        out_specs=pl.BlockSpec(memory_space=pltpu.VMEM),
        scratch_shapes=[
            pltpu.VMEM((rows, LANES), f32),
            pltpu.VMEM((NZ, NX * rows + 8, LANES), f32),
            pltpu.VMEM((depth, width), f32),
            pltpu.VMEM((depth, width), bf16),
            pltpu.VMEM((depth, width), bf16),
            pltpu.VMEM((64, depth), bf16),
            pltpu.VMEM((NZ, 32, width), f32),
            pltpu.VMEM((2, PEERS, 32, width), f32),
            pltpu.VMEM((NX * NR, width), f32),
            pltpu.VMEM((NX * NR, width), f32),
            dma,
            dma((2, NZ, 2)),
            dma((NZ, 2)),
            dma((2, NZ, 2)),
            dma((2, NZ, 2)),
            dma((2, NZ)),
            dma((2, NZ)),
            dma((NZ,)),
            dma((2, PEERS)),
            dma,
            dma,
        ],
        compiler_params=pltpu.CompilerParams(
            collective_id=0, has_side_effects=True, vmem_limit_bytes=40 * 1024 * 1024),
        cost_estimate=pl.CostEstimate(
            flops=6 * 512 * depth * width, bytes_accessed=4 * depth * width, transcendentals=0),
        name="ladder",
    )(amplitudes, integrals)


def per_device(amplitudes, integrals, direct_terms, occ_energy, virt_energy):
    ladder = ladder_rows(amplitudes, integrals)
    denominator = occ_energy[:, None] - virt_energy[None, :]
    return (0.5 * ladder + direct_terms) / denominator


def solution(mesh):
    in_specs = (P("col", "row"), P("row", "col"), P("row", "col"), P("row"), P("col"))
    out_specs = P("row", "col")
    return jax.shard_map(
        per_device, mesh=mesh, in_specs=in_specs, out_specs=out_specs, check_vma=False
    )
```

```python
import functools

import jax
import jax.numpy as jnp
from jax import lax
from jax.experimental import pallas as pl
from jax.experimental.pallas import tpu as pltpu
from jax.sharding import PartitionSpec as P

MESH = pl.DeviceIdType.MESH
NX = 4
NZ = 16
NR = 5
LANES = 128
PEERS = 8


def kernel(n_chunks, amp_ref, b_hbm, out_ref, own, slabs, b_raw, b_hi, b_lo, lhs, part, part_in, cross, cross_in,
           b_sem, z_send, z_recv, x_send, x_recv, f_send, f_recv, p_send, p_recv, c_send, c_recv, here_sem):
    rows = own.shape[0]
    half = rows // 2
    row = lax.axis_index("row")
    col = lax.axis_index("col")
    x, z = lax.rem(col, NX), col // NX
    zh, me8 = row // PEERS, lax.rem(row, PEERS)
    right = z * NX + lax.rem(x + 1, NX)
    left = z * NX + lax.rem(x + NX - 1, NX)
    x_left, x_right, x_far = lax.rem(x + 3, NX), lax.rem(x + 1, NX), lax.rem(x + 2, NX)

    b_copy = pltpu.make_async_copy(b_hbm, b_raw, b_sem)
    b_copy.start()

    partner = (1 - zh) * PEERS + me8
    barrier = pltpu.get_barrier_semaphore()

    def greet(r, c):
        pl.semaphore_signal(barrier, inc=1, device_id={"row": r, "col": c}, device_id_type=MESH)

    greet(row, left)
    greet(row, right)
    for d in range(1, PEERS):
        greet(zh * PEERS + lax.rem(me8 + d, PEERS), col)

    for d in (1, 2):
        @pl.when(z >= d)
        def _():
            greet(row, col - d * NX)

        @pl.when(z < NZ - d)
        def _():
            greet(row, col + d * NX)

    @pl.when(zh == 0)
    def _():
        greet(PEERS + me8, x)

    for k in range(n_chunks):
        own[k * NR : (k + 1) * NR, :] = amp_ref[:, k * LANES : (k + 1) * LANES]
    if n_chunks * NR < rows:
        own[n_chunks * NR :, :] = jnp.zeros((rows - n_chunks * NR, LANES), jnp.float32)
    slabs[z, pl.ds(pl.multiple_of(x * rows, 8), rows), :] = own[...]

    near = 1 + PEERS + jnp.where((zh == 1) & (z == 0), NZ, 0)
    for d in (1, 2):
        near = near + jnp.where(z >= d, 1, 0) + jnp.where(z < NZ - d, 1, 0)
    pl.semaphore_wait(barrier, near)

    def piece(zs, xs, p):
        return slabs.at[zs, pl.ds(pl.multiple_of(xs * rows + p * half, 8), half), :]

    def z_copy(zs, up, d):
        to = jnp.minimum(col + d * NX, NZ * NX - 1) if up else jnp.maximum(col - d * NX, 0)
        ref = slabs.at[zs, pl.ds(pl.multiple_of(x * rows, 8), rows), :]
        return pltpu.make_async_remote_copy(ref, ref, z_send.at[up, d - 1, zs], z_recv.at[zs],
                                            device_id={"row": row, "col": to}, device_id_type=MESH)

    def x_copy(zs, p, to_right):
        ref = piece(zs, x, p)
        return pltpu.make_async_remote_copy(ref, ref, x_send.at[to_right, zs, p], x_recv.at[to_right, zs, p],
                                            device_id={"row": row, "col": right if to_right else left},
                                            device_id_type=MESH)

    def x_arrival(zs, p, to_right):
        ref = piece(zs, x_left if to_right else x_right, p)
        return pltpu.make_async_copy(ref, ref, x_recv.at[to_right, zs, p])

    def f_copy(zs, to_right):
        ref = piece(zs, x_left if to_right else x_right, 1 - to_right)
        return pltpu.make_async_remote_copy(ref, ref, f_send.at[to_right, zs], f_recv.at[to_right, zs],
                                            device_id={"row": row, "col": right if to_right else left},
                                            device_id_type=MESH)

    def f_arrival(zs, to_right):
        ref = piece(zs, x_far, 1 - to_right)
        return pltpu.make_async_copy(ref, ref, f_recv.at[to_right, zs])

    def p_copy(zs):
        to = zh * PEERS + lax.rem(zs, PEERS)
        return pltpu.make_async_remote_copy(part.at[zs], part_in.at[zs // PEERS, me8], p_send.at[zs],
                                            p_recv.at[zs // PEERS, me8],
                                            device_id={"row": to, "col": col}, device_id_type=MESH)

    def order(n):
        low_first = jnp.where(n <= z, z - n, n)
        high_first = jnp.where(n < NZ - z, z + n, NZ - 1 - n)
        return jnp.where(zh == 1, low_first, high_first)

    def z_start(zs, up):
        for d in (2, 1):
            @pl.when((z < NZ - d) if up else (z >= d))
            def _():
                z_copy(zs, up, d).start()

    def z_step(t):
        for o in (2 * t, 2 * t - 1):
            onward = lax.rem(o, 2) == 0

            @pl.when(z - o >= 0)
            def _():
                z_copy(z - o, 1, 1).wait_recv()

            @pl.when((z - o >= 0) & onward)
            def _():
                z_start(z - o, 1)

            @pl.when(z + o < NZ)
            def _():
                z_copy(z + o, 0, 1).wait_recv()

            @pl.when((z + o < NZ) & onward)
            def _():
                z_start(z + o, 0)

    def x_start(zs):
        x_copy(zs, 0, 1).start()
        x_copy(zs, 1, 0).start()
        x_copy(zs, 1, 1).start()
        x_copy(zs, 0, 0).start()

    def x_forward(zs):
        x_arrival(zs, 0, 1).wait()
        f_copy(zs, 1).start()
        x_arrival(zs, 1, 0).wait()
        f_copy(zs, 0).start()

    def finish(zs):
        x_arrival(zs, 1, 1).wait()
        x_arrival(zs, 0, 0).wait()
        f_arrival(zs, 1).wait()
        f_arrival(zs, 0).wait()
        for q in range(NX // 2):
            for k in range(n_chunks):
                v = jnp.concatenate(
                    [slabs[zs, (2 * q + i) * rows + k * NR : (2 * q + i) * rows + k * NR + 8, :] for i in range(2)],
                    axis=0)
                hi = v.astype(jnp.bfloat16)
                lo = (v - hi.astype(jnp.float32)).astype(jnp.bfloat16)
                lhs[16 * q : 16 * q + 16, k * LANES : (k + 1) * LANES] = hi
                lhs[32 + 16 * q : 48 + 16 * q, k * LANES : (k + 1) * LANES] = lo
        both = jnp.dot(lhs[...], b_hi[...], preferred_element_type=jnp.float32)
        cross_term = jnp.dot(lhs[:32, :], b_lo[...], preferred_element_type=jnp.float32)
        part[zs] = both[:32] + (both[32:] + cross_term)

        @pl.when(lax.rem(zs, PEERS) != me8)
        def _():
            p_copy(zs).start()

    def total(h):
        s = part[h * PEERS + me8]
        for d in range(1, PEERS):
            q = lax.rem(me8 + d, PEERS)
            ref = part_in.at[h, q]
            pltpu.make_async_copy(ref, ref, p_recv.at[h, q]).wait()
            s = s + part_in[h, q]
        return jnp.concatenate([s[8 * i : 8 * i + NR, :] for i in range(NX)], axis=0)

    c_copy = pltpu.make_async_remote_copy(cross, cross_in, c_send, c_recv,
                                          device_id={"row": partner, "col": col}, device_id_type=MESH)
    theirs = (1 - zh) * PEERS + me8

    told = jnp.maximum((z + 1) // 2, 1)
    due = jnp.maximum((jnp.where(me8 <= z, z - me8, me8) + 7) // 2, told)

    z_start(z, 1)
    z_start(z, 0)
    x_start(z)

    b_copy.wait()
    depth = b_raw.shape[0]

    @pl.loop(0, depth // 256)
    def _(i):
        at = pl.ds(pl.multiple_of(i * 256, 256), 256)
        v = b_raw[at, :]
        hi = v.astype(jnp.bfloat16)
        b_hi[at, :] = hi
        b_lo[at, :] = (v - hi.astype(jnp.float32)).astype(jnp.bfloat16)

    @pl.loop(1, NZ // 2 + 4)
    def _(t):
        z_step(t)
        for n in (2 * t - 1, 2 * t):
            @pl.when(n < NZ)
            def _():
                x_start(order(n))

        for n in (2 * t - 3, 2 * t - 2):
            @pl.when((n >= 0) & (n < NZ))
            def _():
                x_forward(order(n))

        for n in (2 * t - 5, 2 * t - 4):
            @pl.when((n >= 0) & (n < NZ))
            def _():
                finish(order(n))

        @pl.when((zh == 1) & (t == told))
        def _():
            pl.semaphore_signal(here_sem, inc=1, device_id={"row": partner, "col": col}, device_id_type=MESH)

        @pl.when((zh == 1) & (t == due))
        def _():
            cross[...] = total(1 - zh)
            c_copy.start()

    @pl.when(zh == 0)
    def _():
        pl.semaphore_wait(here_sem, 1)
        cross[...] = total(1 - zh)
        c_copy.start()

    mine = total(zh)
    c_copy.wait_recv()
    out_ref[...] = mine + cross_in[...]
    c_copy.wait_send()

    @pl.loop(0, NZ)
    def _(zs):
        even = lax.rem(z + zs, 2) == 0
        for d in (1, 2):
            @pl.when((z < NZ - d) & (zs <= z) & even)
            def _():
                z_copy(zs, 1, d).wait_send()

            @pl.when((z >= d) & (zs >= z) & even)
            def _():
                z_copy(zs, 0, d).wait_send()

        for p in range(2):
            for to_right in range(2):
                x_copy(zs, p, to_right).wait_send()
        for to_right in range(2):
            f_copy(zs, to_right).wait_send()

        @pl.when(lax.rem(zs, PEERS) != me8)
        def _():
            p_copy(zs).wait_send()


def ladder_rows(amplitudes, integrals):
    depth, width = integrals.shape
    n_chunks = depth // LANES
    rows = -(-n_chunks * NR // 16) * 16
    f32, bf16 = jnp.float32, jnp.bfloat16
    dma = pltpu.SemaphoreType.DMA
    return pl.pallas_call(
        functools.partial(kernel, n_chunks),
        out_shape=jax.ShapeDtypeStruct((NX * NR, width), f32),
        in_specs=[pl.BlockSpec(memory_space=pltpu.VMEM), pl.BlockSpec(memory_space=pl.ANY)],
        out_specs=pl.BlockSpec(memory_space=pltpu.VMEM),
        scratch_shapes=[
            pltpu.VMEM((rows, LANES), f32),
            pltpu.VMEM((NZ, NX * rows + 8, LANES), f32),
            pltpu.VMEM((depth, width), f32),
            pltpu.VMEM((depth, width), bf16),
            pltpu.VMEM((depth, width), bf16),
            pltpu.VMEM((64, depth), bf16),
            pltpu.VMEM((NZ, 32, width), f32),
            pltpu.VMEM((2, PEERS, 32, width), f32),
            pltpu.VMEM((NX * NR, width), f32),
            pltpu.VMEM((NX * NR, width), f32),
            dma,
            dma((2, 2, NZ)),
            dma((NZ,)),
            dma((2, NZ, 2)),
            dma((2, NZ, 2)),
            dma((2, NZ)),
            dma((2, NZ)),
            dma((NZ,)),
            dma((2, PEERS)),
            dma,
            dma,
            pltpu.SemaphoreType.REGULAR,
        ],
        compiler_params=pltpu.CompilerParams(
            collective_id=0, has_side_effects=True, vmem_limit_bytes=60 * 1024 * 1024),
        cost_estimate=pl.CostEstimate(
            flops=6 * 512 * depth * width, bytes_accessed=4 * depth * width, transcendentals=0),
        name="ladder",
    )(amplitudes, integrals)


def per_device(amplitudes, integrals, direct_terms, occ_energy, virt_energy):
    ladder = ladder_rows(amplitudes, integrals)
    denominator = occ_energy[:, None] - virt_energy[None, :]
    return (0.5 * ladder + direct_terms) / denominator


def solution(mesh):
    in_specs = (P("col", "row"), P("row", "col"), P("row", "col"), P("row"), P("col"))
    out_specs = P("row", "col")
    return jax.shard_map(
        per_device, mesh=mesh, in_specs=in_specs, out_specs=out_specs, check_vma=False
    )
```

```python
import functools

import jax
import jax.numpy as jnp
from jax import lax
from jax.experimental import pallas as pl
from jax.experimental.pallas import tpu as pltpu
from jax.sharding import PartitionSpec as P

MESH = pl.DeviceIdType.MESH
NX = 4
NZ = 16
NR = 5
LANES = 128
LAST = 2
PEERS = 8


def kernel(n_chunks, amp_hbm, b_hbm, out_ref, amp, own, slabs, b_raw, b_hi, b_lo, lhs, part, part_in, cross, cross_in,
           a_sem, b_sem, z_send, z_recv, x_send, x_recv, f_send, f_recv, p_send, p_recv, c_send, c_recv, here_sem):
    rows = own.shape[0]
    half = rows // 2
    row = lax.axis_index("row")
    col = lax.axis_index("col")
    x, z = lax.rem(col, NX), col // NX
    zh, me8 = row // PEERS, lax.rem(row, PEERS)
    right = z * NX + lax.rem(x + 1, NX)
    left = z * NX + lax.rem(x + NX - 1, NX)
    x_left, x_right, x_far = lax.rem(x + 3, NX), lax.rem(x + 1, NX), lax.rem(x + 2, NX)

    a_copy = pltpu.make_async_copy(amp_hbm, amp, a_sem)
    a_copy.start()
    b_copy = pltpu.make_async_copy(b_hbm, b_raw, b_sem)
    b_copy.start()

    partner = (1 - zh) * PEERS + me8
    barrier = pltpu.get_barrier_semaphore()

    def greet(r, c):
        pl.semaphore_signal(barrier, inc=1, device_id={"row": r, "col": c}, device_id_type=MESH)

    greet(row, left)
    greet(row, right)
    for d in range(1, PEERS):
        greet(zh * PEERS + lax.rem(me8 + d, PEERS), col)

    for d in (1, 2):
        @pl.when(z >= d)
        def _():
            greet(row, col - d * NX)

        @pl.when(z < NZ - d)
        def _():
            greet(row, col + d * NX)

    @pl.when(zh == 0)
    def _():
        greet(PEERS + me8, x)

    a_copy.wait()
    for k in range(n_chunks):
        own[k * NR : (k + 1) * NR, :] = amp[:, k * LANES : (k + 1) * LANES]
    if n_chunks * NR < rows:
        own[n_chunks * NR :, :] = jnp.zeros((rows - n_chunks * NR, LANES), jnp.float32)
    slabs[z, pl.ds(pl.multiple_of(x * rows, 8), rows), :] = own[...]

    near = 1 + PEERS + jnp.where((zh == 1) & (z == 0), NZ, 0)
    for d in (1, 2):
        near = near + jnp.where(z >= d, 1, 0) + jnp.where(z < NZ - d, 1, 0)
    pl.semaphore_wait(barrier, near)

    def piece(zs, xs, p):
        return slabs.at[zs, pl.ds(pl.multiple_of(xs * rows + p * half, 8), half), :]

    def z_device(up, d):
        to = jnp.minimum(col + d * NX, NZ * NX - 1) if up else jnp.maximum(col - d * NX, 0)
        return {"row": row, "col": to}

    def z_far(zs, up, p):
        ref = piece(zs, x, p)
        return pltpu.make_async_remote_copy(ref, ref, z_send.at[up, p, zs], z_recv.at[zs, p],
                                            device_id=z_device(up, 2), device_id_type=MESH)

    def z_near(zs, up):
        ref = slabs.at[zs, pl.ds(pl.multiple_of(x * rows, 8), rows), :]
        return pltpu.make_async_remote_copy(ref, ref, z_send.at[up, 2, zs], z_recv.at[zs, 0],
                                            device_id=z_device(up, 1), device_id_type=MESH)

    def x_copy(zs, p, to_right):
        ref = piece(zs, x, p)
        return pltpu.make_async_remote_copy(ref, ref, x_send.at[to_right, zs, p], x_recv.at[to_right, zs, p],
                                            device_id={"row": row, "col": right if to_right else left},
                                            device_id_type=MESH)

    def x_arrival(zs, p, to_right):
        ref = piece(zs, x_left if to_right else x_right, p)
        return pltpu.make_async_copy(ref, ref, x_recv.at[to_right, zs, p])

    def f_copy(zs, to_right):
        ref = piece(zs, x_left if to_right else x_right, 1 - to_right)
        return pltpu.make_async_remote_copy(ref, ref, f_send.at[to_right, zs], f_recv.at[to_right, zs],
                                            device_id={"row": row, "col": right if to_right else left},
                                            device_id_type=MESH)

    def far_copy(zs, to_right):
        ref = piece(zs, x, 1 - to_right)
        return pltpu.make_async_remote_copy(ref, ref, f_send.at[to_right, zs], f_recv.at[to_right, zs],
                                            device_id={"row": row, "col": z * NX + x_far}, device_id_type=MESH)

    def f_arrival(zs, to_right):
        ref = piece(zs, x_far, 1 - to_right)
        return pltpu.make_async_copy(ref, ref, f_recv.at[to_right, zs])

    def p_copy(zs):
        to = zh * PEERS + lax.rem(zs, PEERS)
        return pltpu.make_async_remote_copy(part.at[zs], part_in.at[zs // PEERS, me8], p_send.at[zs],
                                            p_recv.at[zs // PEERS, me8],
                                            device_id={"row": to, "col": col}, device_id_type=MESH)

    def order(n):
        low_first = jnp.where(n <= z, z - n, n)
        high_first = jnp.where(n < NZ - z, z + n, NZ - 1 - n)
        return jnp.where(zh == 1, low_first, high_first)

    def far_start(zs, up, p):
        @pl.when((z < NZ - 2) if up else (z >= 2))
        def _():
            z_far(zs, up, p).start()

    def near_start(zs, up):
        @pl.when((z < NZ - 1) if up else (z >= 1))
        def _():
            z_near(zs, up).start()

    def z_step(t):
        below, above = z - 2 * t, z + 2 * t
        for p in range(2):
            @pl.when(below >= 0)
            def _():
                z_far(below, 1, p).wait_recv()
                far_start(below, 1, p)

            @pl.when(above < NZ)
            def _():
                z_far(above, 0, p).wait_recv()
                far_start(above, 0, p)

        @pl.when(below >= 0)
        def _():
            near_start(below, 1)

        @pl.when(above < NZ)
        def _():
            near_start(above, 0)

        @pl.when(below + 1 >= 0)
        def _():
            z_near(below + 1, 1).wait_recv()

        @pl.when(above - 1 < NZ)
        def _():
            z_near(above - 1, 0).wait_recv()

    def x_start(n):
        zs = order(n)

        @pl.when(n >= NZ - LAST)
        def _():
            far_copy(zs, 1).start()
            far_copy(zs, 0).start()

        x_copy(zs, 0, 1).start()
        x_copy(zs, 1, 0).start()
        x_copy(zs, 1, 1).start()
        x_copy(zs, 0, 0).start()

    def x_forward(n):
        zs = order(n)
        x_arrival(zs, 0, 1).wait()
        x_arrival(zs, 1, 0).wait()

        @pl.when(n < NZ - LAST)
        def _():
            f_copy(zs, 1).start()
            f_copy(zs, 0).start()

    def finish(zs):
        x_arrival(zs, 1, 1).wait()
        x_arrival(zs, 0, 0).wait()
        f_arrival(zs, 1).wait()
        f_arrival(zs, 0).wait()
        for q in range(NX // 2):
            for k in range(n_chunks):
                v = jnp.concatenate(
                    [slabs[zs, (2 * q + i) * rows + k * NR : (2 * q + i) * rows + k * NR + 8, :] for i in range(2)],
                    axis=0)
                hi = v.astype(jnp.bfloat16)
                lo = (v - hi.astype(jnp.float32)).astype(jnp.bfloat16)
                lhs[16 * q : 16 * q + 16, k * LANES : (k + 1) * LANES] = hi
                lhs[32 + 16 * q : 48 + 16 * q, k * LANES : (k + 1) * LANES] = lo
        both = jnp.dot(lhs[...], b_hi[...], preferred_element_type=jnp.float32)
        cross_term = jnp.dot(lhs[:32, :], b_lo[...], preferred_element_type=jnp.float32)
        part[zs] = both[:32] + (both[32:] + cross_term)

        @pl.when(lax.rem(zs, PEERS) != me8)
        def _():
            p_copy(zs).start()

    def total(h):
        s = part[h * PEERS + me8]
        for d in range(1, PEERS):
            q = lax.rem(me8 + d, PEERS)
            ref = part_in.at[h, q]
            pltpu.make_async_copy(ref, ref, p_recv.at[h, q]).wait()
            s = s + part_in[h, q]
        return jnp.concatenate([s[8 * i : 8 * i + NR, :] for i in range(NX)], axis=0)

    c_copy = pltpu.make_async_remote_copy(cross, cross_in, c_send, c_recv,
                                          device_id={"row": partner, "col": col}, device_id_type=MESH)

    told = jnp.maximum((z + 1) // 2, 1)
    high = PEERS + me8
    turn = jnp.where(zh == 1, jnp.where(me8 <= z, z - me8, me8), jnp.where(high >= z, high - z, NZ - 1 - high))
    due = jnp.maximum((turn + 9) // 2, jnp.where(zh == 1, told, NZ // 2 + z // 5))

    for p in range(2):
        far_start(z, 1, p)
        far_start(z, 0, p)
    near_start(z, 1)
    near_start(z, 0)
    x_start(0)

    b_copy.wait()
    depth = b_raw.shape[0]

    @pl.loop(0, depth // 256)
    def _(i):
        at = pl.ds(pl.multiple_of(i * 256, 256), 256)
        v = b_raw[at, :]
        hi = v.astype(jnp.bfloat16)
        b_hi[at, :] = hi
        b_lo[at, :] = (v - hi.astype(jnp.float32)).astype(jnp.bfloat16)

    @pl.loop(1, NZ // 2 + 5)
    def _(t):
        z_step(t)
        for n in (2 * t - 1, 2 * t):
            @pl.when(n < NZ)
            def _():
                x_start(n)

        for n in (2 * t - 7, 2 * t - 6):
            @pl.when((n >= 0) & (n < NZ))
            def _():
                finish(order(n))

        for n in (2 * t - 3, 2 * t - 2):
            @pl.when((n >= 0) & (n < NZ))
            def _():
                x_forward(n)

        @pl.when((zh == 1) & (t == told))
        def _():
            pl.semaphore_signal(here_sem, inc=1, device_id={"row": partner, "col": col}, device_id_type=MESH)

        @pl.when((zh == 0) & (t == due))
        def _():
            pl.semaphore_wait(here_sem, 1)

        @pl.when(t == due)
        def _():
            cross[...] = total(1 - zh)
            c_copy.start()

    @pl.loop(0, NZ)
    def _(zs):
        even = lax.rem(z + zs, 2) == 0
        for up in range(2):
            passed = even & ((zs <= z) if up else (zs >= z))
            for p in range(2):
                @pl.when(passed & ((z < NZ - 2) if up else (z >= 2)))
                def _():
                    z_far(zs, up, p).wait_send()

            @pl.when(passed & ((z < NZ - 1) if up else (z >= 1)))
            def _():
                z_near(zs, up).wait_send()

        for p in range(2):
            for to_right in range(2):
                x_copy(zs, p, to_right).wait_send()
        for to_right in range(2):
            f_copy(zs, to_right).wait_send()

        @pl.when(lax.rem(zs, PEERS) != me8)
        def _():
            p_copy(zs).wait_send()

    mine = total(zh)
    c_copy.wait_recv()
    out_ref[...] = mine + cross_in[...]
    c_copy.wait_send()


def ladder_rows(amplitudes, integrals):
    depth, width = integrals.shape
    n_chunks = depth // LANES
    rows = -(-n_chunks * NR // 16) * 16
    f32, bf16 = jnp.float32, jnp.bfloat16
    dma = pltpu.SemaphoreType.DMA
    return pl.pallas_call(
        functools.partial(kernel, n_chunks),
        out_shape=jax.ShapeDtypeStruct((NX * NR, width), f32),
        in_specs=[pl.BlockSpec(memory_space=pl.ANY)] * 2,
        out_specs=pl.BlockSpec(memory_space=pltpu.VMEM),
        scratch_shapes=[
            pltpu.VMEM(amplitudes.shape, f32),
            pltpu.VMEM((rows, LANES), f32),
            pltpu.VMEM((NZ, NX * rows + 8, LANES), f32),
            pltpu.VMEM((depth, width), f32),
            pltpu.VMEM((depth, width), bf16),
            pltpu.VMEM((depth, width), bf16),
            pltpu.VMEM((64, depth), bf16),
            pltpu.VMEM((NZ, 32, width), f32),
            pltpu.VMEM((2, PEERS, 32, width), f32),
            pltpu.VMEM((NX * NR, width), f32),
            pltpu.VMEM((NX * NR, width), f32),
            dma,
            dma,
            dma((2, 3, NZ)),
            dma((NZ, 2)),
            dma((2, NZ, 2)),
            dma((2, NZ, 2)),
            dma((2, NZ)),
            dma((2, NZ)),
            dma((NZ,)),
            dma((2, PEERS)),
            dma,
            dma,
            pltpu.SemaphoreType.REGULAR,
        ],
        compiler_params=pltpu.CompilerParams(
            collective_id=0, has_side_effects=True, vmem_limit_bytes=60 * 1024 * 1024),
        cost_estimate=pl.CostEstimate(
            flops=6 * 512 * depth * width, bytes_accessed=4 * depth * width, transcendentals=0),
        name="ladder",
    )(amplitudes, integrals)


def per_device(amplitudes, integrals, direct_terms, occ_energy, virt_energy):
    ladder = ladder_rows(amplitudes, integrals)
    denominator = occ_energy[:, None] - virt_energy[None, :]
    return (0.5 * ladder + direct_terms) / denominator


def solution(mesh):
    in_specs = (P("col", "row"), P("row", "col"), P("row", "col"), P("row"), P("col"))
    out_specs = P("row", "col")
    return jax.shard_map(
        per_device, mesh=mesh, in_specs=in_specs, out_specs=out_specs, check_vma=False
    )
```

```python
import functools

import jax
import jax.numpy as jnp
from jax import lax
from jax.experimental import pallas as pl
from jax.experimental.pallas import tpu as pltpu
from jax.sharding import PartitionSpec as P

MESH = pl.DeviceIdType.MESH
NX = 4
NZ = 16
NR = 5
LANES = 128
HUB = 2
LAST = 4
PEERS = 8


def kernel(n_chunks, amp_hbm, b_hbm, out_ref, amp, own, slabs, b_raw, b_hi, b_lo, lhs, part, part_in, cross, cross_in,
           a_sem, b_sem, z_send, z_recv, x_send, x_recv, f_send, f_recv, p_send, p_recv, c_send, c_recv, here_sem):
    rows = own.shape[0]
    half = rows // 2
    row = lax.axis_index("row")
    col = lax.axis_index("col")
    x, z = lax.rem(col, NX), col // NX
    zh, me8 = row // PEERS, lax.rem(row, PEERS)
    right = z * NX + lax.rem(x + 1, NX)
    left = z * NX + lax.rem(x + NX - 1, NX)
    x_left, x_right, x_far = lax.rem(x + 3, NX), lax.rem(x + 1, NX), lax.rem(x + 2, NX)

    a_copy = pltpu.make_async_copy(amp_hbm, amp, a_sem)
    a_copy.start()
    b_copy = pltpu.make_async_copy(b_hbm, b_raw, b_sem)
    b_copy.start()

    partner = (1 - zh) * PEERS + me8
    barrier = pltpu.get_barrier_semaphore()

    def greet(r, c):
        pl.semaphore_signal(barrier, inc=1, device_id={"row": r, "col": c}, device_id_type=MESH)

    greet(row, left)
    greet(row, right)
    for d in range(1, PEERS):
        greet(zh * PEERS + lax.rem(me8 + d, PEERS), col)

    for d in (1, 2):
        @pl.when(z >= d)
        def _():
            greet(row, col - d * NX)

        @pl.when(z < NZ - d)
        def _():
            greet(row, col + d * NX)

    @pl.when(zh == 0)
    def _():
        greet(PEERS + me8, jnp.minimum(z, HUB) * NX + x)

    a_copy.wait()
    for k in range(n_chunks):
        own[k * NR : (k + 1) * NR, :] = amp[:, k * LANES : (k + 1) * LANES]
    if n_chunks * NR < rows:
        own[n_chunks * NR :, :] = jnp.zeros((rows - n_chunks * NR, LANES), jnp.float32)
    slabs[z, pl.ds(pl.multiple_of(x * rows, 8), rows), :] = own[...]

    near = 1 + PEERS + jnp.where(zh == 1, jnp.where(z < HUB, 1, jnp.where(z == HUB, NZ - HUB, 0)), 0)
    for d in (1, 2):
        near = near + jnp.where(z >= d, 1, 0) + jnp.where(z < NZ - d, 1, 0)
    pl.semaphore_wait(barrier, near)

    def piece(zs, xs, p):
        return slabs.at[zs, pl.ds(pl.multiple_of(xs * rows + p * half, 8), half), :]

    def z_device(up, d):
        to = jnp.minimum(col + d * NX, NZ * NX - 1) if up else jnp.maximum(col - d * NX, 0)
        return {"row": row, "col": to}

    def z_far(zs, up, p):
        ref = piece(zs, x, p)
        return pltpu.make_async_remote_copy(ref, ref, z_send.at[up, p, zs], z_recv.at[zs, p],
                                            device_id=z_device(up, 2), device_id_type=MESH)

    def z_near(zs, up):
        ref = slabs.at[zs, pl.ds(pl.multiple_of(x * rows, 8), rows), :]
        return pltpu.make_async_remote_copy(ref, ref, z_send.at[up, 2, zs], z_recv.at[zs, 0],
                                            device_id=z_device(up, 1), device_id_type=MESH)

    def x_copy(zs, p, to_right):
        ref = piece(zs, x, p)
        return pltpu.make_async_remote_copy(ref, ref, x_send.at[to_right, zs, p], x_recv.at[to_right, zs, p],
                                            device_id={"row": row, "col": right if to_right else left},
                                            device_id_type=MESH)

    def x_arrival(zs, p, to_right):
        ref = piece(zs, x_left if to_right else x_right, p)
        return pltpu.make_async_copy(ref, ref, x_recv.at[to_right, zs, p])

    def f_copy(zs, to_right):
        ref = piece(zs, x_left if to_right else x_right, 1 - to_right)
        return pltpu.make_async_remote_copy(ref, ref, f_send.at[to_right, zs], f_recv.at[to_right, zs],
                                            device_id={"row": row, "col": right if to_right else left},
                                            device_id_type=MESH)

    def far_copy(zs, to_right):
        ref = piece(zs, x, 1 - to_right)
        return pltpu.make_async_remote_copy(ref, ref, f_send.at[to_right, zs], f_recv.at[to_right, zs],
                                            device_id={"row": row, "col": z * NX + x_far}, device_id_type=MESH)

    def f_arrival(zs, to_right):
        ref = piece(zs, x_far, 1 - to_right)
        return pltpu.make_async_copy(ref, ref, f_recv.at[to_right, zs])

    def p_copy(zs):
        to = zh * PEERS + lax.rem(zs, PEERS)
        return pltpu.make_async_remote_copy(part.at[zs], part_in.at[zs // PEERS, me8], p_send.at[zs],
                                            p_recv.at[zs // PEERS, me8],
                                            device_id={"row": to, "col": col}, device_id_type=MESH)

    def order(n):
        low_first = jnp.where(n <= z, z - n, n)
        high_first = jnp.where(n < NZ - z, z + n, NZ - 1 - n)
        return jnp.where(zh == 1, low_first, high_first)

    def far_start(zs, up, p):
        @pl.when((z < NZ - 2) if up else (z >= 2))
        def _():
            z_far(zs, up, p).start()

    def near_start(zs, up):
        @pl.when((z < NZ - 1) if up else (z >= 1))
        def _():
            z_near(zs, up).start()

    def z_step(t):
        below, above = z - 2 * t, z + 2 * t
        for p in range(2):
            @pl.when(below >= 0)
            def _():
                z_far(below, 1, p).wait_recv()
                far_start(below, 1, p)

            @pl.when(above < NZ)
            def _():
                z_far(above, 0, p).wait_recv()
                far_start(above, 0, p)

        @pl.when(below >= 0)
        def _():
            near_start(below, 1)

        @pl.when(above < NZ)
        def _():
            near_start(above, 0)

        @pl.when(below + 1 >= 0)
        def _():
            z_near(below + 1, 1).wait_recv()

        @pl.when(above - 1 < NZ)
        def _():
            z_near(above - 1, 0).wait_recv()

    def x_start(n):
        zs = order(n)

        @pl.when(n >= NZ - LAST)
        def _():
            far_copy(zs, 1).start()
            far_copy(zs, 0).start()

        x_copy(zs, 0, 1).start()
        x_copy(zs, 1, 0).start()
        x_copy(zs, 1, 1).start()
        x_copy(zs, 0, 0).start()

    def x_forward(n):
        zs = order(n)
        x_arrival(zs, 0, 1).wait()
        x_arrival(zs, 1, 0).wait()

        @pl.when(n < NZ - LAST)
        def _():
            f_copy(zs, 1).start()
            f_copy(zs, 0).start()

    def finish(zs):
        x_arrival(zs, 1, 1).wait()
        x_arrival(zs, 0, 0).wait()
        f_arrival(zs, 1).wait()
        f_arrival(zs, 0).wait()
        for q in range(NX // 2):
            for k in range(n_chunks):
                v = jnp.concatenate(
                    [slabs[zs, (2 * q + i) * rows + k * NR : (2 * q + i) * rows + k * NR + 8, :] for i in range(2)],
                    axis=0)
                hi = v.astype(jnp.bfloat16)
                lo = (v - hi.astype(jnp.float32)).astype(jnp.bfloat16)
                lhs[16 * q : 16 * q + 16, k * LANES : (k + 1) * LANES] = hi
                lhs[32 + 16 * q : 48 + 16 * q, k * LANES : (k + 1) * LANES] = lo
        both = jnp.dot(lhs[...], b_hi[...], preferred_element_type=jnp.float32)
        cross_term = jnp.dot(lhs[:32, :], b_lo[...], preferred_element_type=jnp.float32)
        part[zs] = both[:32] + (both[32:] + cross_term)

        @pl.when(lax.rem(zs, PEERS) != me8)
        def _():
            p_copy(zs).start()

    def total(h):
        s = part[h * PEERS + me8]
        for d in range(1, PEERS):
            q = lax.rem(me8 + d, PEERS)
            ref = part_in.at[h, q]
            pltpu.make_async_copy(ref, ref, p_recv.at[h, q]).wait()
            s = s + part_in[h, q]
        return jnp.concatenate([s[8 * i : 8 * i + NR, :] for i in range(NX)], axis=0)

    c_copy = pltpu.make_async_remote_copy(cross, cross_in, c_send, c_recv,
                                          device_id={"row": partner, "col": col}, device_id_type=MESH)

    told = jnp.maximum((z + 1 - HUB) // 2, 1)
    high = PEERS + me8
    turn = jnp.where(zh == 1, jnp.where(me8 <= z, z - me8, me8), jnp.where(high >= z, high - z, NZ - 1 - high))
    due = jnp.maximum((turn + 7) // 2, jnp.where(zh == 1, told, (25 + 4 * told - z) // 4 + 1))

    for p in range(2):
        far_start(z, 1, p)
        far_start(z, 0, p)
    near_start(z, 1)
    near_start(z, 0)
    x_start(0)

    b_copy.wait()
    depth = b_raw.shape[0]

    @pl.loop(0, depth // 256)
    def _(i):
        at = pl.ds(pl.multiple_of(i * 256, 256), 256)
        v = b_raw[at, :]
        hi = v.astype(jnp.bfloat16)
        b_hi[at, :] = hi
        b_lo[at, :] = (v - hi.astype(jnp.float32)).astype(jnp.bfloat16)

    @pl.loop(1, NZ // 2 + 4)
    def _(t):
        z_step(t)
        for n in (2 * t - 1, 2 * t):
            @pl.when(n < NZ)
            def _():
                x_start(n)

        for n in (2 * t - 3, 2 * t - 2):
            @pl.when((n >= 0) & (n < NZ))
            def _():
                x_forward(n)

        for n in (2 * t - 5, 2 * t - 4):
            @pl.when((n >= 0) & (n < NZ))
            def _():
                finish(order(n))

        @pl.when((zh == 1) & (t == told))
        def _():
            pl.semaphore_signal(here_sem, inc=1, device_id={"row": partner, "col": col}, device_id_type=MESH)

        @pl.when((zh == 0) & (t == due))
        def _():
            pl.semaphore_wait(here_sem, 1)

        @pl.when(t == due)
        def _():
            cross[...] = total(1 - zh)
            c_copy.start()

    @pl.loop(0, NZ)
    def _(zs):
        even = lax.rem(z + zs, 2) == 0
        for up in range(2):
            passed = even & ((zs <= z) if up else (zs >= z))
            for p in range(2):
                @pl.when(passed & ((z < NZ - 2) if up else (z >= 2)))
                def _():
                    z_far(zs, up, p).wait_send()

            @pl.when(passed & ((z < NZ - 1) if up else (z >= 1)))
            def _():
                z_near(zs, up).wait_send()

        for p in range(2):
            for to_right in range(2):
                x_copy(zs, p, to_right).wait_send()
        for to_right in range(2):
            f_copy(zs, to_right).wait_send()

        @pl.when(lax.rem(zs, PEERS) != me8)
        def _():
            p_copy(zs).wait_send()

    mine = total(zh)
    c_copy.wait_recv()
    out_ref[...] = mine + cross_in[...]
    c_copy.wait_send()


def ladder_rows(amplitudes, integrals):
    depth, width = integrals.shape
    n_chunks = depth // LANES
    rows = -(-n_chunks * NR // 16) * 16
    f32, bf16 = jnp.float32, jnp.bfloat16
    dma = pltpu.SemaphoreType.DMA
    return pl.pallas_call(
        functools.partial(kernel, n_chunks),
        out_shape=jax.ShapeDtypeStruct((NX * NR, width), f32),
        in_specs=[pl.BlockSpec(memory_space=pl.ANY)] * 2,
        out_specs=pl.BlockSpec(memory_space=pltpu.VMEM),
        scratch_shapes=[
            pltpu.VMEM(amplitudes.shape, f32),
            pltpu.VMEM((rows, LANES), f32),
            pltpu.VMEM((NZ, NX * rows + 8, LANES), f32),
            pltpu.VMEM((depth, width), f32),
            pltpu.VMEM((depth, width), bf16),
            pltpu.VMEM((depth, width), bf16),
            pltpu.VMEM((64, depth), bf16),
            pltpu.VMEM((NZ, 32, width), f32),
            pltpu.VMEM((2, PEERS, 32, width), f32),
            pltpu.VMEM((NX * NR, width), f32),
            pltpu.VMEM((NX * NR, width), f32),
            dma,
            dma,
            dma((2, 3, NZ)),
            dma((NZ, 2)),
            dma((2, NZ, 2)),
            dma((2, NZ, 2)),
            dma((2, NZ)),
            dma((2, NZ)),
            dma((NZ,)),
            dma((2, PEERS)),
            dma,
            dma,
            pltpu.SemaphoreType.REGULAR,
        ],
        compiler_params=pltpu.CompilerParams(
            collective_id=0, has_side_effects=True, vmem_limit_bytes=60 * 1024 * 1024),
        cost_estimate=pl.CostEstimate(
            flops=6 * 512 * depth * width, bytes_accessed=4 * depth * width, transcendentals=0),
        name="ladder",
    )(amplitudes, integrals)


def per_device(amplitudes, integrals, direct_terms, occ_energy, virt_energy):
    ladder = ladder_rows(amplitudes, integrals)
    denominator = occ_energy[:, None] - virt_energy[None, :]
    return (0.5 * ladder + direct_terms) / denominator


def solution(mesh):
    in_specs = (P("col", "row"), P("row", "col"), P("row", "col"), P("row"), P("col"))
    out_specs = P("row", "col")
    return jax.shard_map(
        per_device, mesh=mesh, in_specs=in_specs, out_specs=out_specs, check_vma=False
    )
```
